256 devices in a mesh: seq: 64 (over y, z, core), head: 4 (over x).
Axes of the slice: x: 4, y: 4, z: 8, core: 2. Of those that a mesh axis runs over, the one named last changes fastest.
Arguments:
- queries: bfloat16 [16384, 32, 128], P(('seq', 'head')), may hold values from -16 to 16
- key_states: bfloat16 [16384, 4, 128], P(('seq', 'head')), may hold values from -8 to 8
- value_states: bfloat16 [16384, 4, 128], P(('seq', 'head')), may hold values from -6 to 6
- out_grad: bfloat16 [16384, 32, 128], P(('seq', 'head')), may hold values from -6 to 6
- doc_lengths: int32 [8], replicated, may hold values from 1 to 8192, 16384 in all
Outputs:
- attended: bfloat16 [16384, 32, 128], P(('seq', 'head'))
- query_grad: bfloat16 [16384, 32, 128], P(('seq', 'head'))
- key_grad: bfloat16 [16384, 4, 128], P(('seq', 'head'))
- value_grad: bfloat16 [16384, 4, 128], P(('seq', 'head'))
The draws below stay inside these ranges and needn't reach their ends.
Inputs may be any that keep to these rules, and one draw needn't show every extreme that they name: `doc_lengths`: the 8 lengths sum to 16384; documents follow one another in the pack in this order.
All inputs are finite; a program needn't handle non-finite values.
Results may differ from the reference program's by a relative error of at most 0.035.
Values may be sent and summed in bfloat16 or wider, within the bound.
No kernel may reach another device: no remote copies, remote signals or barrier semaphores. Data moves between devices by JAX's collectives and lax.ppermute only.
A program may use at most 64 MiB of HBM per device.

```python
import math
import jax
import jax.numpy as jnp
import numpy as np
from jax import lax

HD = 128
GROUP_HEADS = 8
KV_GROUPS = 4
QHEADS = 32
SHARD_TOK = 256
TOKENS = 16384
REACH = 32
DOC_MOST = 8192
DOCS = 8


def draw_queries(key, part):
    key = jax.random.fold_in(key, 5)
    normal_part = jax.random.normal(key, (TOKENS, QHEADS, HD), jnp.float32)
    result = jnp.clip(normal_part, -6.0, 6.0)
    return result.astype(jnp.bfloat16)


def draw_key_states(key, part):
    key = jax.random.fold_in(key, 7)
    normal_part = jax.random.normal(key, (TOKENS, KV_GROUPS, HD), jnp.float32)
    result = jnp.clip(normal_part, -6.0, 6.0)
    return result.astype(jnp.bfloat16)


def levels(key, dims, pieces, smallest, high):
    def one(position, parts):
        draws = jax.random.uniform(jax.random.fold_in(jax.random.fold_in(key, 6), position), (parts,), jnp.float32, smallest / len(pieces), high / len(pieces))
        return jnp.repeat(jnp.exp(draws), dims[position] // parts).reshape((-1,) + (1,) * (len(dims) - position - 1))

    level = one(*pieces[0])
    for cut in pieces[1:]:
        level = level * one(*cut)
    return level


def profile(count, total, most, lean):
    weights = [(1 << 20) // math.isqrt(grade ** lean) + 1 for grade in range(2, count + 1)]
    spare, holding = total - most - (count - 1), [1] * (count - 1)
    while spare > 0:
        movable = [i for i in range(count - 1) if holding[i] < most]
        pool, left = sum([weights[i] for i in movable]), spare
        for i in movable:
            addition = min(most - holding[i], max(1, left * weights[i] // pool), spare)
            holding[i] = holding[i] + addition
            spare = spare - addition
    return np.array([most] + holding)


def uneven_parts(own_key, number_of, total, most, lean):
    if number_of == 2:
        one = jax.random.randint(own_key, (), max(1, total - most), min(most, total - 1) + 1)
        return jnp.stack([one, total - one])
    lengths = jnp.asarray(profile(number_of, total, most, lean), jnp.int32)
    couples = (number_of - 1) // 2
    donor, receiver = lengths[1:1 + 2 * couples:2], lengths[2:2 + 2 * couples:2]
    room = jnp.minimum(donor - 1, most - receiver)
    passed = jax.random.randint(jax.random.fold_in(own_key, 1), (couples,), 0, 1 << 20) % (room + 1)
    lengths = lengths.at[1:1 + 2 * couples:2].set(donor - passed).at[2:2 + 2 * couples:2].set(receiver + passed)
    return lengths[jax.random.permutation(jax.random.fold_in(own_key, 2), number_of)]


def normal_values(rng, extent, spread, limit, split=(), kind=jnp.bfloat16):
    entries = spread * jax.random.normal(rng, extent, jnp.float32)
    if split:
        entries = entries * levels(rng, extent, split, -0.22, 0.18)
    return jnp.clip(entries, -limit, limit).astype(kind)


def setup_inputs(seed: int = 0) -> dict:
    key_list = jax.random.split(jax.random.key(seed), 6)
    return {
        "queries": draw_queries(jax.random.fold_in(key_list[5], 71), 0),
        "key_states": draw_key_states(jax.random.fold_in(key_list[5], 71), 0),
        "value_states": normal_values(key_list[2], (TOKENS, KV_GROUPS, HD), 1.0, 6.0, ((0, 256),)),
        "out_grad": normal_values(key_list[3], (TOKENS, QHEADS, HD), 1.0, 6.0, ((0, 256),)),
        "doc_lengths": uneven_parts(key_list[4], DOCS, TOKENS, DOC_MOST, 2).astype(jnp.int32),
    }


def reference(queries, key_states, value_states, out_grad, doc_lengths):
    blk_rows = SHARD_TOK
    lead_rows = REACH * blk_rows
    inv_root = HD ** -0.5
    doc_ends = jnp.cumsum(doc_lengths).astype(jnp.int32)
    positions = jnp.arange(TOKENS, dtype=jnp.int32)
    doc_ids = jnp.sum((positions[:, None] >= doc_ends[None, :]).astype(jnp.int32), axis=1).astype(jnp.int32)
    ids_pad = jnp.concatenate([jnp.full((lead_rows,), -1, jnp.int32), doc_ids])
    tile_list = jnp.arange(REACH + 1, dtype=jnp.int32)
    outs_all, dq_all, dk_all, dv_all = [], [], [], []
    for kv_group in range(KV_GROUPS):
        q_group = queries[:, kv_group * GROUP_HEADS:(kv_group + 1) * GROUP_HEADS, :]
        g_group = out_grad[:, kv_group * GROUP_HEADS:(kv_group + 1) * GROUP_HEADS, :]
        k_pad = jnp.concatenate([jnp.zeros((lead_rows, HD), jnp.bfloat16), key_states[:, kv_group, :]])
        v_pad = jnp.concatenate([jnp.zeros((lead_rows, HD), jnp.bfloat16), value_states[:, kv_group, :]])

        def block_step(acc_pair, blk_index):
            dk_acc, dv_acc = acc_pair
            q_start = (blk_index * blk_rows).astype(jnp.int32)
            q_blk = lax.dynamic_slice_in_dim(q_group, q_start, blk_rows, 0).astype(jnp.float32)
            g_blk = lax.dynamic_slice_in_dim(g_group, q_start, blk_rows, 0).astype(jnp.float32)
            q_ids = lax.dynamic_slice_in_dim(doc_ids, q_start, blk_rows, 0)
            q_pos = q_start + jnp.arange(blk_rows, dtype=jnp.int32)

            def tile_of(tile):
                pad_start = (q_start + lead_rows - tile * blk_rows).astype(jnp.int32)
                k_tile = lax.dynamic_slice_in_dim(k_pad, pad_start, blk_rows, 0).astype(jnp.float32)
                v_tile = lax.dynamic_slice_in_dim(v_pad, pad_start, blk_rows, 0).astype(jnp.float32)
                id_tile = lax.dynamic_slice_in_dim(ids_pad, pad_start, blk_rows, 0)
                k_pos = pad_start - lead_rows + jnp.arange(blk_rows, dtype=jnp.int32)
                allowed = (id_tile[None, :] == q_ids[:, None]) & (k_pos[None, :] <= q_pos[:, None]) & (id_tile[None, :] >= 0)
                return pad_start, k_tile, v_tile, allowed

            def scores_of(k_tile):
                return jnp.einsum("thd,ud->htu", q_blk, k_tile) * inv_root

            def keep(running):
                return running

            def stats_step(running, tile):
                pad_start, k_tile, v_tile, allowed = tile_of(tile)

                def update(state):
                    row_top, row_total = state
                    scores = scores_of(k_tile)
                    new_top = jnp.maximum(row_top, jnp.max(jnp.where(allowed[None], scores, -jnp.inf), axis=-1))
                    new_total = row_total * jnp.exp(row_top - new_top) + jnp.sum(jnp.where(allowed[None], jnp.exp(scores - new_top[:, :, None]), 0.0), axis=-1)
                    return new_top, new_total

                return lax.cond(jnp.any(allowed), update, keep, running), None

            top_start = jnp.full((GROUP_HEADS, blk_rows), -jnp.inf, jnp.float32)
            total_start = jnp.zeros((GROUP_HEADS, blk_rows), jnp.float32)
            (row_top, row_total), _ = lax.scan(stats_step, (top_start, total_start), tile_list)

            def weights_of(k_tile, allowed):
                scores = scores_of(k_tile)
                return jnp.where(allowed[None], jnp.exp(scores - row_top[:, :, None]), 0.0) / row_total[:, :, None]

            def out_step(running, tile):
                pad_start, k_tile, v_tile, allowed = tile_of(tile)

                def add_tile(acc):
                    weights_b = lax.optimization_barrier(weights_of(k_tile, allowed).astype(jnp.bfloat16)).astype(jnp.float32)
                    return acc + jnp.einsum("htu,ud->thd", weights_b, v_tile)

                return lax.cond(jnp.any(allowed), add_tile, keep, running), None

            zero_blk = jnp.zeros((blk_rows, GROUP_HEADS, HD), jnp.float32)
            out_sum, _ = lax.scan(out_step, zero_blk, tile_list)
            out_blk = out_sum.astype(jnp.bfloat16)
            row_dot = jnp.sum(g_blk * out_blk.astype(jnp.float32), axis=-1).T

            def grad_step(running, tile):
                pad_start, k_tile, v_tile, allowed = tile_of(tile)

                def work(state):
                    dq_run, dk_run, dv_run = state
                    weights = weights_of(k_tile, allowed)
                    weights_b = lax.optimization_barrier(weights.astype(jnp.bfloat16)).astype(jnp.float32)
                    prob_grad = jnp.einsum("thd,ud->htu", g_blk, v_tile)
                    score_b = lax.optimization_barrier((weights * (prob_grad - row_dot[:, :, None])).astype(jnp.bfloat16)).astype(jnp.float32)
                    dq_run = dq_run + jnp.einsum("htu,ud->thd", score_b, k_tile)
                    dk_tile = jnp.einsum("htu,thd->ud", score_b, q_blk) * inv_root
                    dv_tile = jnp.einsum("htu,thd->ud", weights_b, g_blk)
                    dk_run = lax.dynamic_update_slice_in_dim(dk_run, lax.dynamic_slice_in_dim(dk_run, pad_start, blk_rows, 0) + dk_tile, pad_start, 0)
                    dv_run = lax.dynamic_update_slice_in_dim(dv_run, lax.dynamic_slice_in_dim(dv_run, pad_start, blk_rows, 0) + dv_tile, pad_start, 0)
                    return dq_run, dk_run, dv_run

                return lax.cond(jnp.any(allowed), work, keep, running), None

            (dq_sum, dk_acc, dv_acc), _ = lax.scan(grad_step, (zero_blk, dk_acc, dv_acc), tile_list)
            dq_blk = (dq_sum * inv_root).astype(jnp.bfloat16)
            return (dk_acc, dv_acc), (out_blk, dq_blk)

        zero_acc = jnp.zeros((TOKENS + lead_rows, HD), jnp.float32)
        (dk_acc, dv_acc), (out_blocks, dq_blocks) = lax.scan(block_step, (zero_acc, zero_acc), jnp.arange(TOKENS // blk_rows, dtype=jnp.int32))
        outs_all.append(out_blocks.reshape(TOKENS, GROUP_HEADS, HD))
        dq_all.append(dq_blocks.reshape(TOKENS, GROUP_HEADS, HD))
        dk_all.append(dk_acc[lead_rows:])
        dv_all.append(dv_acc[lead_rows:])
    attended = jnp.concatenate(outs_all, axis=1)
    query_grad = jnp.concatenate(dq_all, axis=1)
    key_grad = jnp.stack(dk_all, axis=1).astype(jnp.bfloat16)
    value_grad = jnp.stack(dv_all, axis=1).astype(jnp.bfloat16)
    return (attended, query_grad, key_grad, value_grad)
```

```python
import jax
import jax.numpy as jnp
from jax import lax
from jax.experimental import pallas as pl
from jax.experimental.pallas import tpu as pltpu
from jax.sharding import Mesh, PartitionSpec as P

NEG = -1e30
HDIM = 128
CLOG = 1.4426950408889634 * HDIM ** -0.5
INV = HDIM ** -0.5
BF = jnp.bfloat16
UNROLL = 4


def nn(a, b):
    return lax.dot_general(a, b, (((1,), (0,)), ((), ())), preferred_element_type=jnp.float32)


def tn(a, b):
    return lax.dot_general(a, b, (((0,), (0,)), ((), ())), preferred_element_type=jnp.float32)


def kernel(info, q_ref, g_ref, kv_ref, o_ref, dq_ref, da_ref, db_ref, acc, dacc, dacc_kv, stat, qt, gt):
    b = pl.program_id(0)
    nb = pl.num_programs(0)
    rows = q_ref.shape[0]
    nx, toks = kv_ref.shape[1], kv_ref.shape[3]
    kt = nx * toks
    s = 16 * b + info[0]

    def doc_start(pos):
        start = jnp.zeros_like(pos)
        for i in range(8):
            start = jnp.where(pos >= info[2 + i], info[2 + i], start)
        return start

    lane = lax.broadcasted_iota(jnp.int32, (1, rows), 1)
    t = s * kt + (lane // 128) * toks + info[1] * 16 + (lane % 128) // 8
    dstart = doc_start(t)
    lo = doc_start(s * kt) // kt
    mid = jnp.minimum((doc_start(s * kt + kt - 1) + kt - 1) // kt, s)
    sub = lax.broadcasted_iota(jnp.int32, (kt, 1), 0)

    @pl.when(b == 0)
    def _():
        dacc_kv[...] = jnp.zeros_like(dacc_kv)

    acc[...] = jnp.zeros_like(acc)
    dacc[...] = jnp.zeros_like(dacc)
    stat[0:1] = jnp.full((1, rows), NEG, jnp.float32)
    stat[1:2] = jnp.zeros((1, rows), jnp.float32)
    qt[...] = q_ref[...].astype(jnp.float32).T.astype(BF)
    gt[...] = g_ref[...].astype(jnp.float32).T.astype(BF)

    def key(j):
        return kv_ref[j, :, 0].reshape(kt, HDIM)

    def val(j):
        return kv_ref[j, :, 1].reshape(kt, HDIM)

    def allowed(j):
        u = sub + j * kt
        return (u <= t) & (u >= dstart)

    def loop(fn):
        lax.fori_loop(lo, mid, lambda j, c: (fn([j], True), c)[1], 0)
        n = (s - mid) // UNROLL
        lax.fori_loop(0, n, lambda i, c: (fn([mid + i * UNROLL + k for k in range(UNROLL)], False), c)[1], 0)
        lax.fori_loop(mid + n * UNROLL, s, lambda j, c: (fn([j], False), c)[1], 0)
        fn([s], True)

    def fwd(js, masked):
        scores = [nn(key(j), qt[...]) for j in js]
        if masked:
            scores = [jnp.where(allowed(j), sc, NEG) for j, sc in zip(js, scores)]
        old = stat[0:1]
        top = old
        for sc in scores:
            top = jnp.maximum(top, jnp.max(sc, axis=0, keepdims=True))
        fade = jnp.exp2((old - top) * CLOG)
        stat[0:1] = top
        total = stat[1:2] * fade
        out = acc[...] * fade
        for j, sc in zip(js, scores):
            p = jnp.exp2((sc - top) * CLOG)
            total = total + jnp.sum(p, axis=0, keepdims=True)
            out = out + tn(val(j), p.astype(BF))
        stat[1:2] = total
        acc[...] = out

    loop(fwd)
    out_t = acc[...] / stat[1:2]
    lse = stat[0:1] * CLOG + jnp.log2(stat[1:2])
    o_ref[...] = out_t.T.astype(BF)
    dot = jnp.sum(gt[...].astype(jnp.float32) * out_t.astype(BF).astype(jnp.float32), axis=0, keepdims=True)

    def bwd(js, masked):
        for j in js:
            kj, vj = key(j), val(j)
            p = jnp.exp2(nn(kj, qt[...]) * CLOG - lse)
            if masked:
                p = jnp.where(allowed(j), p, 0.0)
            dp = nn(vj, gt[...])
            ds = (p * (dp - dot)).astype(BF)
            dacc[...] += tn(kj, ds)
            dacc_kv[j, 0] += nn(ds, q_ref[...])
            dacc_kv[j, 1] += nn(p.astype(BF), g_ref[...])

    loop(bwd)
    dq_ref[...] = (dacc[...] * INV).T.astype(BF)

    @pl.when(b == nb - 1)
    def _():
        def put(j, carry):
            core, z, y = j % 2, (j // 2) % 8, j // 16
            dk, dv = (dacc_kv[j, 0] * INV).astype(BF), dacc_kv[j, 1].astype(BF)
            half = kt // 2
            da_ref[core, z, y, 0], da_ref[core, z, y, 1] = dk[:half], dv[:half]
            db_ref[core, y, z, 0], db_ref[core, y, z, 1] = dk[half:], dv[half:]
            return carry

        lax.fori_loop(0, kv_ref.shape[0], put, 0)


def attend(info, q, g, kv):
    nb, rows, _ = q.shape
    tiles = kv.shape[0]
    kt = kv.shape[1] * kv.shape[3]
    blk = pl.BlockSpec((None, rows, HDIM), lambda b, info: (b, 0, 0))

    def whole(shape):
        return pl.BlockSpec(shape, lambda b, info: (0,) * len(shape), pipeline_mode=pl.Buffered(1))

    a_shape, b_shape = (2, 8, 4, 2, kt // 2, HDIM), (2, 4, 8, 2, kt // 2, HDIM)
    return pl.pallas_call(
        kernel,
        grid_spec=pltpu.PrefetchScalarGridSpec(
            num_scalar_prefetch=1,
            grid=(nb,),
            in_specs=[blk, blk, whole(kv.shape)],
            out_specs=[blk, blk, whole(a_shape), whole(b_shape)],
            scratch_shapes=[
                pltpu.VMEM((HDIM, rows), jnp.float32),
                pltpu.VMEM((HDIM, rows), jnp.float32),
                pltpu.VMEM((tiles, 2, kt, HDIM), jnp.float32),
                pltpu.VMEM((2, rows), jnp.float32),
                pltpu.VMEM((HDIM, rows), BF),
                pltpu.VMEM((HDIM, rows), BF),
            ],
        ),
        out_shape=[jax.ShapeDtypeStruct(shape, BF) for shape in (q.shape, q.shape, a_shape, b_shape)],
        compiler_params=pltpu.CompilerParams(vmem_limit_bytes=56 * 1024 * 1024),
    )(info, q, g, kv)


SEQ = ("y", "z", "core")
ALL = ("y", "z", "core", "x")
SIZES = {"y": 4, "z": 8, "core": 2, "x": 4}


def shift(value, axis, steps):
    count = SIZES[axis]
    return lax.ppermute(value, axis, [(i, (i + steps) % count) for i in range(count)])


def ring_sum(blocks, axis):
    count = SIZES[axis]
    me = lax.axis_index(axis)

    def own(offset):
        return lax.dynamic_index_in_dim(blocks, lax.rem(me + offset + count, count), 0, keepdims=False)

    far = count // 2
    half = blocks.shape[1] // 2
    start = own(far)
    right, left = start[:half], start[half:]
    for offset in range(far - 1, 0, -1):
        from_left, from_right = shift(right, axis, 1), shift(left, axis, -1)
        right, left = own(offset), own(-offset)
        if offset == far - 1:
            right = jnp.concatenate([right[:half] + from_left, right[half:]])
            left = jnp.concatenate([left[:half], left[half:] + from_right])
        else:
            right, left = right + from_left, left + from_right
    from_left, from_right = shift(right, axis, 1), shift(left, axis, -1)
    return f32(own(0)) + f32(from_left) + f32(from_right)


def f32(value):
    return value.astype(jnp.float32)


def shards(queries, key_states, value_states, out_grad, doc_lengths):
    ends = jnp.cumsum(doc_lengths)
    spot = 2 * lax.axis_index("z") + lax.axis_index("core")
    info = jnp.concatenate([jnp.stack([spot, lax.axis_index("y")]), ends]).astype(jnp.int32)

    kv = jnp.stack([key_states, value_states]).transpose(2, 0, 1, 3)
    kv = lax.all_to_all(kv, "x", 0, 0)
    kv = lax.all_gather(kv, SEQ, axis=0)

    def spread(value):
        value = value.reshape(4, 16, 4, 8, HDIM).transpose(0, 2, 1, 3, 4).reshape(16, 16, 8, HDIM)
        return lax.all_to_all(value, ("y", "x"), 0, 0).reshape(4, 512, HDIM)

    def home(value):
        value = lax.all_to_all(value.reshape(16, 16, 8, HDIM), ("y", "x"), 0, 0)
        return value.reshape(4, 4, 16, 8, HDIM).transpose(0, 2, 1, 3, 4).reshape(64, 32, HDIM)

    out, dq, part_a, part_b = attend(info, spread(queries), spread(out_grad), kv)
    core = lax.axis_index("core")

    def join_cores(part):
        mine = lax.dynamic_index_in_dim(part, core, 0, keepdims=False)
        other = lax.dynamic_index_in_dim(part, 1 - core, 0, keepdims=False)
        return mine + shift(other, "core", 1)

    part_a = ring_sum(join_cores(part_a), "z").astype(jnp.bfloat16)
    part_b = ring_sum(join_cores(part_b), "y").astype(jnp.bfloat16)
    part_a = ring_sum(part_a, "y")
    part_b = ring_sum(part_b, "z")
    dkv = jnp.concatenate([part_a, part_b], axis=1).astype(jnp.bfloat16).reshape(2, 4, 64, HDIM)
    dkv = lax.all_to_all(dkv, "x", 1, 0)
    return home(out), home(dq), dkv[:, 0].transpose(1, 0, 2), dkv[:, 1].transpose(1, 0, 2)


def solution(mesh):
    fine = Mesh(mesh.devices.reshape(4, 8, 2, 4), ALL)
    return jax.shard_map(
        shards,
        mesh=fine,
        in_specs=(P(ALL), P(ALL), P(ALL), P(ALL), P()),
        out_specs=(P(ALL), P(ALL), P(ALL), P(ALL)),
        check_vma=False,
    )
```

```python
import jax
import jax.numpy as jnp
from jax import lax
from jax.experimental import pallas as pl
from jax.experimental.pallas import tpu as pltpu
from jax.sharding import Mesh, PartitionSpec as P

NEG = -1e30
HDIM = 128
CLOG = 1.4426950408889634 * HDIM ** -0.5
INV = HDIM ** -0.5
BF = jnp.bfloat16
UNROLL = 4
ROWS = 512
TILE = 256
SIZES = {"y": 4, "z": 8, "core": 2, "x": 4}


def nn(a, b):
    return lax.dot_general(a, b, (((1,), (0,)), ((), ())), preferred_element_type=jnp.float32)


def tn(a, b):
    return lax.dot_general(a, b, (((0,), (0,)), ((), ())), preferred_element_type=jnp.float32)


def landing():
    near = [(steps, 0, 4) for steps in range(4)] + [(-steps, 0, 4) for steps in range(1, 4)]
    return near + [(4, 0, 2), (4, 2, 4)]


def kernel(info, qg_ref, *refs):
    places = [(other, place) for other in (0, 1) for place in landing()]
    kv_in, refs = refs[: len(places)], refs[len(places):]
    od_ref, mine, others, refs = refs[0], refs[1:9], refs[9:17], refs[17:]
    acc, dacc, dkv, stat, qt, gt, qs, gs, kv, sems = refs
    b = pl.program_id(0)
    nb = pl.num_programs(0)
    spot, me_y, me_z, me_core = info[0], info[1], info[2], info[3]
    s = 16 * b + spot

    def doc_start(pos):
        start = jnp.zeros_like(pos)
        for i in range(8):
            start = jnp.where(pos >= info[4 + i], info[4 + i], start)
        return start

    lane = lax.broadcasted_iota(jnp.int32, (1, ROWS), 1)
    t = s * TILE + (lane // 128) * 64 + me_y * 16 + (lane % 128) // 8
    dstart = doc_start(t)
    lo = doc_start(s * TILE) // TILE
    mid = jnp.minimum((doc_start(s * TILE + TILE - 1) + TILE - 1) // TILE, s)
    sub = lax.broadcasted_iota(jnp.int32, (TILE, 1), 0)

    @pl.when(b == 0)
    def _():
        copies = []
        for n, (ref, (other, (back, first, last))) in enumerate(zip(kv_in, places)):
            core = me_core if other == 0 else 1 - me_core
            target = kv.at[pl.ds(first, last - first), lax.rem(me_z - back + 8, 8), core]
            copies.append(pltpu.make_async_copy(ref, target, sems.at[n]))
        for copy in copies:
            copy.start()
        dkv[...] = jnp.zeros_like(dkv)
        for copy in copies:
            copy.wait()

    acc[...] = jnp.zeros_like(acc)
    dacc[...] = jnp.zeros_like(dacc)
    stat[0:1] = jnp.full((1, ROWS), NEG, jnp.float32)
    stat[1:2] = jnp.zeros((1, ROWS), jnp.float32)
    qs[...] = qg_ref[:, 0].reshape(ROWS, HDIM)
    gs[...] = qg_ref[:, 1].reshape(ROWS, HDIM)
    qt[...] = qs[...].astype(jnp.float32).T.astype(BF)
    gt[...] = gs[...].astype(jnp.float32).T.astype(BF)

    def key(j):
        return kv[j // 16, (j // 2) % 8, j % 2, :, 0].reshape(TILE, HDIM)

    def val(j):
        return kv[j // 16, (j // 2) % 8, j % 2, :, 1].reshape(TILE, HDIM)

    def allowed(j):
        u = sub + j * TILE
        return (u <= t) & (u >= dstart)

    def loop(fn):
        lax.fori_loop(lo, mid, lambda j, c: (fn([j], True), c)[1], 0)
        n = (s - mid) // UNROLL
        lax.fori_loop(0, n, lambda i, c: (fn([mid + i * UNROLL + k for k in range(UNROLL)], False), c)[1], 0)
        lax.fori_loop(mid + n * UNROLL, s, lambda j, c: (fn([j], False), c)[1], 0)
        fn([s], True)

    def fwd(js, masked):
        scores = [nn(key(j), qt[...]) for j in js]
        if masked:
            scores = [jnp.where(allowed(j), sc, NEG) for j, sc in zip(js, scores)]
        old = stat[0:1]
        top = old
        for sc in scores:
            top = jnp.maximum(top, jnp.max(sc, axis=0, keepdims=True))
        fade = jnp.exp2((old - top) * CLOG)
        stat[0:1] = top
        total = stat[1:2] * fade
        out = acc[...] * fade
        for j, sc in zip(js, scores):
            p = jnp.exp2((sc - top) * CLOG)
            total = total + jnp.sum(p, axis=0, keepdims=True)
            out = out + tn(val(j), p.astype(BF))
        stat[1:2] = total
        acc[...] = out

    loop(fwd)
    out_t = acc[...] / stat[1:2]
    lse = stat[0:1] * CLOG + jnp.log2(stat[1:2])
    od_ref[:, 0] = out_t.T.astype(BF).reshape(4, 128, HDIM)
    dot = jnp.sum(gt[...].astype(jnp.float32) * out_t.astype(BF).astype(jnp.float32), axis=0, keepdims=True)

    def bwd(js, masked):
        for j in js:
            kj, vj = key(j), val(j)
            p = jnp.exp2(nn(kj, qt[...]) * CLOG - lse)
            if masked:
                p = jnp.where(allowed(j), p, 0.0)
            dp = nn(vj, gt[...])
            ds = (p * (dp - dot)).astype(BF)
            dacc[...] += tn(kj, ds)
            dkv[j, 0] += nn(ds, qs[...])
            dkv[j, 1] += nn(p.astype(BF), gs[...])

    loop(bwd)
    od_ref[:, 1] = (dacc[...] * INV).T.astype(BF).reshape(4, 128, HDIM)

    @pl.when(b == nb - 1)
    def _():
        for step in range(8):
            z = lax.rem(me_z + step, 8)

            def put(y, carry, step=step, z=z):
                for core, ref in ((me_core, mine[step]), (1 - me_core, others[step])):
                    j = 16 * y + 2 * z + core
                    ref[y, :, 0] = (dkv[j, 0] * INV).astype(BF).reshape(4, 64, HDIM)
                    ref[y, :, 1] = dkv[j, 1].astype(BF).reshape(4, 64, HDIM)
                return carry

            lax.fori_loop(0, 4, put, 0)


def attend(info, qg, kv):
    blk = pl.BlockSpec((None, 4, 2, 128, HDIM), lambda b, info: (b, 0, 0, 0, 0))

    def whole(shape):
        return pl.BlockSpec(shape, lambda b, info: (0,) * len(shape), pipeline_mode=pl.Buffered(1))

    part = (4, 4, 2, 64, HDIM)
    return pl.pallas_call(
        kernel,
        grid_spec=pltpu.PrefetchScalarGridSpec(
            num_scalar_prefetch=1,
            grid=(4,),
            in_specs=[blk] + [pl.BlockSpec(memory_space=pl.ANY)] * len(kv),
            out_specs=[blk] + [whole(part)] * 16,
            scratch_shapes=[
                pltpu.VMEM((HDIM, ROWS), jnp.float32),
                pltpu.VMEM((HDIM, ROWS), jnp.float32),
                pltpu.VMEM((64, 2, TILE, HDIM), jnp.float32),
                pltpu.VMEM((2, ROWS), jnp.float32),
                pltpu.VMEM((HDIM, ROWS), BF),
                pltpu.VMEM((HDIM, ROWS), BF),
                pltpu.VMEM((ROWS, HDIM), BF),
                pltpu.VMEM((ROWS, HDIM), BF),
                pltpu.VMEM((4, 8, 2, 4, 2, 64, HDIM), BF),
                pltpu.SemaphoreType.DMA((len(kv),)),
            ],
        ),
        out_shape=[jax.ShapeDtypeStruct(shape, BF) for shape in [qg.shape] + [part] * 16],
        compiler_params=pltpu.CompilerParams(vmem_limit_bytes=52 * 1024 * 1024),
    )(info, qg, *kv)


ALL = ("y", "z", "core", "x")


def shift(value, axis, steps):
    count = SIZES[axis]
    return lax.ppermute(value, axis, [(i, (i + steps) % count) for i in range(count)])


def ring_gather(block):
    rights, lefts = [block], [block]
    for _ in range(3):
        rights.append(shift(rights[-1], "z", 1))
        lefts.append(shift(lefts[-1], "z", -1))
    return rights + lefts[1:] + [shift(rights[-1][:2], "z", 1), shift(lefts[-1][2:], "z", -1)]


def ring_sum(mine, others):
    start = mine[4] + shift(others[4], "core", 1)
    right, left = start[:2], start[2:]
    for offset in (3, 2, 1):
        own_right = mine[offset] + shift(others[offset], "core", 1)
        own_left = mine[8 - offset] + shift(others[8 - offset], "core", 1)
        from_left, from_right = shift(right, "z", 1), shift(left, "z", -1)
        if offset == 3:
            right = jnp.concatenate([own_right[:2] + from_left, own_right[2:]])
            left = jnp.concatenate([own_left[:2], own_left[2:] + from_right])
        else:
            right, left = own_right + from_left, own_left + from_right
    own = mine[0] + shift(others[0], "core", 1)
    return (f32(own) + f32(shift(right, "z", 1)) + f32(shift(left, "z", -1))).astype(BF)


def f32(value):
    return value.astype(jnp.float32)


def shards(queries, key_states, value_states, out_grad, doc_lengths):
    y, z, core = (lax.axis_index(axis) for axis in ("y", "z", "core"))
    info = jnp.concatenate([jnp.stack([2 * z + core, y, z, core]), jnp.cumsum(doc_lengths)]).astype(jnp.int32)

    kv = jnp.stack([key_states, value_states]).transpose(2, 0, 1, 3)
    kv = jnp.broadcast_to(kv[None], (4, 4, 2, 64, HDIM)).reshape(16, 2, 64, HDIM)
    kv = ring_gather(lax.all_to_all(kv, ("y", "x"), 0, 0).reshape(4, 4, 2, 64, HDIM))
    kv = kv + [shift(block, "core", 1) for block in kv]

    qg = jnp.stack([queries.reshape(4, 16, 4, 8, HDIM), out_grad.reshape(4, 16, 4, 8, HDIM)])
    qg = qg.transpose(1, 3, 0, 2, 4, 5).reshape(16, 2, 16, 8, HDIM)
    qg = lax.all_to_all(qg, ("y", "x"), 0, 0).reshape(4, 4, 2, 128, HDIM)

    od, *parts = attend(info, qg, kv)

    od = lax.all_to_all(od.reshape(16, 2, 16, 8, HDIM), ("y", "x"), 0, 0)
    od = od.reshape(4, 4, 2, 16, 8, HDIM).transpose(2, 0, 3, 1, 4, 5).reshape(2, 64, 32, HDIM)

    dkv = ring_sum(parts[:8], parts[8:]).reshape(16, 2, 64, HDIM)
    dkv = lax.all_to_all(dkv, ("y", "x"), 0, 0).reshape(4, 4, 2, 64, HDIM)
    dkv = jnp.sum(f32(dkv), axis=0).astype(BF).transpose(1, 2, 0, 3)
    return od[0], od[1], dkv[0], dkv[1]


def solution(mesh):
    fine = Mesh(mesh.devices.reshape(4, 8, 2, 4), ALL)
    return jax.shard_map(
        shards,
        mesh=fine,
        in_specs=(P(ALL), P(ALL), P(ALL), P(ALL), P()),
        out_specs=(P(ALL), P(ALL), P(ALL), P(ALL)),
        check_vma=False,
    )
```

```python
import jax
import jax.numpy as jnp
from jax import lax
from jax.experimental import pallas as pl
from jax.experimental.pallas import tpu as pltpu
from jax.sharding import Mesh, PartitionSpec as P

NEG = -1e30
HDIM = 128
CLOG = 1.4426950408889634 * HDIM ** -0.5
INV = HDIM ** -0.5
BF = jnp.bfloat16
ROWS = 512
TILE = 256
PAIR = 2 * TILE
SIZES = {"y": 4, "z": 8, "core": 2, "x": 4}
VMEM_LIMIT = 32 * 1024 * 1024


def nn(a, b):
    return lax.dot_general(a, b, (((1,), (0,)), ((), ())), preferred_element_type=jnp.float32)


def tn(a, b):
    return lax.dot_general(a, b, (((0,), (0,)), ((), ())), preferred_element_type=jnp.float32)


def doc_start(info, pos):
    start = jnp.zeros_like(pos)
    for i in range(8):
        start = jnp.where(pos >= info[4 + i], info[4 + i], start)
    return start


def visit(info, sources, step):
    lane = lax.broadcasted_iota(jnp.int32, (1, ROWS), 1)
    sub = lax.broadcasted_iota(jnp.int32, (TILE, 1), 0)
    views = [(m, back, first, count, 0) for m, (back, first, count) in enumerate(sources)]
    if len(views) % 2:
        m, back, first, count, _ = views.pop()
        views += [(m, back, first, count // 2, 0), (m, back, first + count // 2, count // 2, count // 2)]

    def block(b, carry):
        s = 16 * b + info[0]
        t = s * TILE + (lane // 128) * 64 + info[1] * 16 + (lane % 128) // 8
        dstart = doc_start(info, t)
        start = doc_start(info, s * TILE)
        low = start // PAIR
        full = (doc_start(info, s * TILE + TILE - 1) + PAIR - 1) // PAIR
        high = s // 2

        def tile_mask(p, n):
            tile = 2 * p + (info[3] if n == 0 else 1 - info[3])
            u = sub + tile * TILE
            return tile, (u <= t) & (u >= dstart)

        def couple(views):
            zs = [lax.rem(info[2] - view[1] + 8, 8) for view in views]
            begins = [jnp.maximum((low - z + 7) // 8 - view[2], 0) for z, view in zip(zs, views)]
            ends = [jnp.minimum((high - z + 8) // 8 - view[2], view[3]) for z, view in zip(zs, views)]

            def visit_one(i, carry):
                ps = [8 * (i + view[2]) + z for z, view in zip(zs, views)]
                inside = [(i >= begin) & (i < end) for begin, end in zip(begins, ends)]
                plain = [ok & (p >= full) & (p < high) for ok, p in zip(inside, ps)]
                both = plain[0] & plain[1]
                tiles = [[(view[0], i + view[4], n) for n in range(2)] for view in views]
                pl.when(both)(lambda: step(b, tiles[0] + tiles[1], []))
                for k, view in enumerate(views):
                    pl.when(plain[k] & jnp.logical_not(both))(lambda k=k: step(b, tiles[k], []))

                    def edge(k=k, diagonal=view[1] == 0):
                        masks = [tile_mask(ps[k], n) for n in range(2)]
                        if not diagonal:
                            step(b, tiles[k], [mask for _, mask in masks])
                            return
                        need = [(tile <= s) & (tile * TILE + TILE > start) for tile, _ in masks]
                        every = need[0] & need[1]
                        pl.when(every)(lambda: step(b, tiles[k], [mask for _, mask in masks]))
                        for n, (_, mask) in enumerate(masks):
                            pl.when(need[n] & jnp.logical_not(every))(
                                lambda n=n, mask=mask: step(b, [tiles[k][n]], [mask])
                            )

                    pl.when(inside[k] & jnp.logical_not(plain[k]))(edge)
                return carry

            lax.fori_loop(jnp.minimum(begins[0], begins[1]), jnp.maximum(ends[0], ends[1]), visit_one, 0)

        for n in range(0, len(views), 2):
            couple(views[n: n + 2])
        return carry

    lax.fori_loop(0, 4, block, 0)


def join(kvs, tiles, which):
    return jnp.concatenate([kvs[2 * m + n][i, :, which].reshape(TILE, HDIM) for m, i, n in tiles])


def join_masks(masks):
    return jnp.concatenate(masks) if len(masks) > 1 else masks[0]


def fwd_kernel(sources, first, last, info, *refs):
    n = len(sources)
    qt, refs = refs[0], refs[1:]
    if last:
        gt, refs = refs[0], refs[1:]
    if not first:
        acc_in, stat_in, refs = refs[0], refs[1], refs[2:]
    kvs, refs = refs[: 2 * n], refs[2 * n:]
    if last:
        o_ref, row_ref, acc, stat = refs
    else:
        acc, stat = refs
    if first:
        acc[...] = jnp.zeros_like(acc)
        stat[:, 0:1] = jnp.full((4, 1, ROWS), NEG, jnp.float32)
        stat[:, 1:2] = jnp.zeros((4, 1, ROWS), jnp.float32)
    else:
        acc[...] = acc_in[...]
        stat[...] = stat_in[...]

    def step(b, tiles, masks):
        scores = [nn(join(kvs, [tile], 0), qt[b]) for tile in tiles]
        if masks:
            scores = [jnp.where(mask, sc, NEG) for mask, sc in zip(masks, scores)]
        old = stat[b, 0:1]
        top = old
        for sc in scores:
            top = jnp.maximum(top, jnp.max(sc, axis=0, keepdims=True))
        fade = jnp.exp2((old - top) * CLOG)
        stat[b, 0:1] = top
        total = stat[b, 1:2] * fade
        out = acc[b] * fade
        for tile, sc in zip(tiles, scores):
            p = jnp.exp2((sc - top) * CLOG)
            total = total + jnp.sum(p, axis=0, keepdims=True)
            out = out + tn(join(kvs, [tile], 1), p.astype(BF))
        stat[b, 1:2] = total
        acc[b] = out

    visit(info, sources, step)
    if last:
        for b in range(4):
            out_t = acc[b] / stat[b, 1:2]
            o_ref[b] = out_t.T.astype(BF)
            row_ref[b, 0:1] = stat[b, 0:1] * CLOG + jnp.log2(stat[b, 1:2])
            prod = gt[b].astype(jnp.float32) * out_t.astype(BF).astype(jnp.float32)
            row_ref[b, 1:2] = jnp.sum(prod, axis=0, keepdims=True)


def bwd_kernel(sources, first, last, info, q, g, qt, gt, row, *refs):
    n = len(sources)
    if not first:
        dacc_in, refs = refs[0], refs[1:]
    kvs, refs = refs[: 2 * n], refs[2 * n:]
    if last:
        dq_ref, refs = refs[0], refs[1:]
        parts, dacc, dkvs = refs[: 2 * n], refs[2 * n], refs[2 * n + 1:]
    else:
        dacc, parts, dkvs = refs[0], refs[1: 2 * n + 1], refs[2 * n + 1:]
    dacc[...] = jnp.zeros_like(dacc) if first else dacc_in[...]
    for dkv in dkvs:
        dkv[...] = jnp.zeros_like(dkv)

    def step(b, tiles, masks):
        keys, vals = join(kvs, tiles, 0), join(kvs, tiles, 1)
        p = jnp.exp2(nn(keys, qt[b]) * CLOG - row[b, 0:1])
        if masks:
            p = jnp.where(join_masks(masks), p, 0.0)
        ds = (p * (nn(vals, gt[b]) - row[b, 1:2])).astype(BF)
        dacc[b] += tn(keys, ds)
        dk, dv = nn(ds, q[b]), nn(p.astype(BF), g[b])
        for k, (m, i, n) in enumerate(tiles):
            part = slice(k * TILE, (k + 1) * TILE)
            dkvs[m][i, n, 0] += dk[part]
            dkvs[m][i, n, 1] += dv[part]

    visit(info, sources, step)
    for m, (_, _, count) in enumerate(sources):
        def put(i, carry, m=m):
            for n in range(2):
                parts[2 * m + n][i, :, 0] = (dkvs[m][i, n, 0] * INV).astype(BF).reshape(4, 64, HDIM)
                parts[2 * m + n][i, :, 1] = dkvs[m][i, n, 1].astype(BF).reshape(4, 64, HDIM)
            return carry

        lax.fori_loop(0, count, put, 0)
    if last:
        for b in range(4):
            dq_ref[b] = (dacc[b] * INV).T.astype(BF)


def call(body, ins, outs, scratch, work, aliases={}):
    return pl.pallas_call(
        body,
        in_specs=[pl.BlockSpec(memory_space=pltpu.SMEM)] + [pl.BlockSpec(memory_space=pltpu.VMEM)] * (len(ins) - 1),
        out_specs=[pl.BlockSpec(memory_space=pltpu.VMEM)] * len(outs),
        out_shape=[jax.ShapeDtypeStruct(shape, dtype) for shape, dtype in outs],
        scratch_shapes=[pltpu.VMEM(shape, jnp.float32) for shape in scratch],
        compiler_params=pltpu.CompilerParams(vmem_limit_bytes=VMEM_LIMIT),
        input_output_aliases=aliases,
        cost_estimate=pl.CostEstimate(flops=work, bytes_accessed=4 << 20, transcendentals=0),
    )(*ins)


def fwd_part(info, qt, gt, state, blocks, last):
    sources = [(back, start, own.shape[0]) for back, start, own, _ in blocks]
    tiles = [ref for block in blocks for ref in block[2:]]
    kept = [((4, HDIM, ROWS), jnp.float32), ((4, 2, ROWS), jnp.float32)]
    outs = [((4, ROWS, HDIM), BF), kept[1]] if last else kept
    first = not state

    def body(*refs):
        fwd_kernel(sources, first, last, *refs)

    ins = [info, qt] + ([gt] if last else []) + list(state) + tiles
    return call(body, ins, outs, [shape for shape, _ in kept] if last else [], len(blocks) * 3_500_000_000,
                {2 + n: n for n in range(len(state))} if not last else {})


def bwd_part(info, q, g, qt, gt, row, state, blocks, last):
    sources = [(back, start, own.shape[0]) for back, start, own, _ in blocks]
    tiles = [ref for block in blocks for ref in block[2:]]
    acc = ((4, HDIM, ROWS), jnp.float32)
    parts = [(ref.shape, BF) for ref in tiles]
    sums = [(count, 2, 2, TILE, HDIM) for _, _, count in sources]
    first = not state

    def body(*refs):
        bwd_kernel(sources, first, last, *refs)

    outs = [((4, ROWS, HDIM), BF) if last else acc] + parts
    ins = [info, q, g, qt, gt, row] + list(state) + tiles
    return call(body, ins, outs, ([acc[0]] if last else []) + sums, len(blocks) * 5_000_000_000,
                {6: 0} if state and not last else {})


ALL = ("y", "z", "core", "x")
FWD_GROUPS = ((1, -1, 0), (2, -2), (3, -3))


def shift(value, axis, steps):
    count = SIZES[axis]
    return lax.ppermute(value, axis, [(i, (i + steps) % count) for i in range(count)])


def swap(value):
    return shift(value, "core", 1)


after = lax.optimization_barrier


def f32(value):
    return value.astype(jnp.float32)


def by_owner(value):
    return value.reshape(4, 16, 4, 8, HDIM).transpose(0, 2, 1, 3, 4).reshape(16, 128, HDIM)


def by_token(value):
    return value.reshape(4, 4, 16, 8, HDIM).transpose(0, 2, 1, 3, 4).reshape(64, 32, HDIM)


def shards(queries, key_states, value_states, out_grad, doc_lengths):
    y, z, core = (lax.axis_index(axis) for axis in ("y", "z", "core"))
    info = jnp.concatenate([jnp.stack([2 * z + core, y, z, core]), jnp.cumsum(doc_lengths)]).astype(jnp.int32)

    kv = jnp.stack([key_states, value_states]).transpose(2, 0, 1, 3)
    kv = jnp.broadcast_to(kv[None], (4, 4, 2, 64, HDIM)).reshape(16, 128, HDIM)
    own = lax.all_to_all(kv, ("y", "x"), 0, 0).reshape(4, 4, 2, 64, HDIM)
    q, g = by_owner(queries), by_owner(out_grad)

    blocks, state = {0: [(0, 0, own, swap(own))]}, []
    right = left = own
    for steps in (1, 2, 3, 4):
        if steps < 4:
            right, left = shift(right, "z", 1), shift(left, "z", -1)
        else:
            right, left = shift(right[:2], "z", 1), shift(left[2:], "z", -1)
        if steps == 1:
            q = lax.all_to_all(q, ("y", "x"), 0, 0)
            right, left, q = after((right, left, q))
            q = q.reshape(4, ROWS, HDIM)
            qt = q.transpose(0, 2, 1)
        else:
            chosen = [block for back in FWD_GROUPS[steps - 2] for block in blocks[back]]
            state = fwd_part(info, qt, None, state, chosen, False)
            if steps == 3:
                g = lax.all_to_all(g, ("y", "x"), 0, 0)
            right, left, state, g = after((right, left, state, g))
        if steps < 4:
            blocks[steps] = [(steps, 0, right, swap(right))]
            blocks[-steps] = [(-steps, 0, left, swap(left))]
        else:
            blocks[4] = [(4, 0, right, swap(right)), (4, 2, left, swap(left))]
    g = g.reshape(4, ROWS, HDIM)
    gt = g.transpose(0, 2, 1)
    out, row = fwd_part(info, qt, gt, state, blocks[4], True)
    out = out.reshape(16, 128, HDIM)

    def work(group, state, last):
        chosen = [block for steps in group for block in blocks[steps if steps == 4 else -steps]]
        state, *sums = bwd_part(info, q, g, qt, gt, row, state, chosen, last)
        return [state], sums[0::2], sums[1::2]

    state, mine, others = work((4,), [], False)
    right, left = mine[0] + swap(others[0]), mine[1] + swap(others[1])
    state, right, left = after((state, right, left))
    for steps in (3, 2, 1):
        from_left, from_right = shift(right, "z", 1), shift(left, "z", -1)
        group = (steps, -steps) if steps > 1 else (1, -1, 0)
        state, mine, others = work(group, state, steps == 1)
        state, others, from_left, from_right = after((state, others, from_left, from_right))
        right, left = mine[0] + swap(others[0]), mine[1] + swap(others[1])
        if steps == 3:
            right = jnp.concatenate([right[:2] + from_left, right[2:]])
            left = jnp.concatenate([left[:2], left[2:] + from_right])
        else:
            right, left = right + from_left, left + from_right
        state, right, left = after((state, right, left))
    from_left, from_right = shift(right, "z", 1), shift(left, "z", -1)
    here = mine[2] + swap(others[2])
    done = jnp.concatenate([out, state[0].reshape(16, 128, HDIM)], axis=1)
    done = lax.all_to_all(done, ("y", "x"), 0, 0)
    done, from_left, from_right = after((done, from_left, from_right))
    out, dq = by_token(done[:, :128]), by_token(done[:, 128:])

    dkv = (f32(here) + f32(from_left) + f32(from_right)).astype(BF).reshape(16, 2, 64, HDIM)
    dkv = lax.all_to_all(dkv, ("y", "x"), 0, 0).reshape(4, 4, 2, 64, HDIM)
    dkv = jnp.sum(f32(dkv), axis=0).astype(BF).transpose(1, 2, 0, 3)
    return out, dq, dkv[0], dkv[1]


def solution(mesh):
    fine = Mesh(mesh.devices.reshape(4, 8, 2, 4), ALL)
    return jax.shard_map(
        shards,
        mesh=fine,
        in_specs=(P(ALL), P(ALL), P(ALL), P(ALL), P()),
        out_specs=(P(ALL), P(ALL), P(ALL), P(ALL)),
        check_vma=False,
    )
```

```python
import jax
import jax.numpy as jnp
from jax import lax
from jax.experimental import pallas as pl
from jax.experimental.pallas import tpu as pltpu
from jax.sharding import Mesh, PartitionSpec as P

NEG = -1e30
HDIM = 128
CLOG = 1.4426950408889634 * HDIM ** -0.5
INV = HDIM ** -0.5
BF = jnp.bfloat16
ROWS = 512
TILE = 256
PAIR = 2 * TILE
SIZES = {"y": 4, "z": 8, "core": 2, "x": 4}
VMEM_LIMIT = 32 * 1024 * 1024


def nn(a, b):
    return lax.dot_general(a, b, (((1,), (0,)), ((), ())), preferred_element_type=jnp.float32)


def tn(a, b):
    return lax.dot_general(a, b, (((0,), (0,)), ((), ())), preferred_element_type=jnp.float32)


def doc_start(info, pos):
    start = jnp.zeros_like(pos)
    for i in range(8):
        start = jnp.where(pos >= info[4 + i], info[4 + i], start)
    return start


def visit(info, sources, step):
    lane = lax.broadcasted_iota(jnp.int32, (1, ROWS), 1)
    sub = lax.broadcasted_iota(jnp.int32, (TILE, 1), 0)
    views = [(m, back, first, count, 0) for m, (back, first, count) in enumerate(sources)]
    if len(views) % 2:
        m, back, first, count, _ = views.pop()
        views += [(m, back, first, count // 2, 0), (m, back, first + count // 2, count // 2, count // 2)]

    def block(b, carry):
        s = 16 * b + info[0]
        t = s * TILE + (lane // 128) * 64 + info[1] * 16 + (lane % 128) // 8
        dstart = doc_start(info, t)
        start = doc_start(info, s * TILE)
        low = start // PAIR
        full = (doc_start(info, s * TILE + TILE - 1) + PAIR - 1) // PAIR
        high = s // 2

        def tile_mask(p, n):
            tile = 2 * p + (info[3] if n == 0 else 1 - info[3])
            u = sub + tile * TILE
            return tile, (u <= t) & (u >= dstart)

        def couple(views):
            zs = [lax.rem(info[2] - view[1] + 8, 8) for view in views]
            begins = [jnp.maximum((low - z + 7) // 8 - view[2], 0) for z, view in zip(zs, views)]
            ends = [jnp.minimum((high - z + 8) // 8 - view[2], view[3]) for z, view in zip(zs, views)]

            def visit_one(i, carry):
                ps = [8 * (i + view[2]) + z for z, view in zip(zs, views)]
                inside = [(i >= begin) & (i < end) for begin, end in zip(begins, ends)]
                plain = [ok & (p >= full) & (p < high) for ok, p in zip(inside, ps)]
                both = plain[0] & plain[1]
                tiles = [[(view[0], i + view[4], n) for n in range(2)] for view in views]
                pl.when(both)(lambda: step(b, tiles[0] + tiles[1], []))
                for k, view in enumerate(views):
                    pl.when(plain[k] & jnp.logical_not(both))(lambda k=k: step(b, tiles[k], []))

                    def edge(k=k, diagonal=view[1] == 0):
                        masks = [tile_mask(ps[k], n) for n in range(2)]
                        if not diagonal:
                            step(b, tiles[k], [mask for _, mask in masks])
                            return
                        need = [(tile <= s) & (tile * TILE + TILE > start) for tile, _ in masks]
                        every = need[0] & need[1]
                        pl.when(every)(lambda: step(b, tiles[k], [mask for _, mask in masks]))
                        for n, (_, mask) in enumerate(masks):
                            pl.when(need[n] & jnp.logical_not(every))(
                                lambda n=n, mask=mask: step(b, [tiles[k][n]], [mask])
                            )

                    pl.when(inside[k] & jnp.logical_not(plain[k]))(edge)
                return carry

            lax.fori_loop(jnp.minimum(begins[0], begins[1]), jnp.maximum(ends[0], ends[1]), visit_one, 0)

        for n in range(0, len(views), 2):
            couple(views[n: n + 2])
        return carry

    lax.fori_loop(0, 4, block, 0)


def join(kvs, tiles, which):
    return jnp.concatenate([kvs[2 * m + n][i, :, which].reshape(TILE, HDIM) for m, i, n in tiles])


def join_masks(masks):
    return jnp.concatenate(masks) if len(masks) > 1 else masks[0]


def fwd_kernel(sources, first, last, info, *refs):
    n = len(sources)
    qt, refs = refs[0], refs[1:]
    if last:
        gt, refs = refs[0], refs[1:]
    if not first:
        acc_in, stat_in, refs = refs[0], refs[1], refs[2:]
    kvs, refs = refs[: 2 * n], refs[2 * n:]
    if last:
        o_ref, row_ref, acc, stat = refs
    else:
        acc, stat = refs
    if first:
        acc[...] = jnp.zeros_like(acc)
        stat[:, 0:1] = jnp.full((4, 1, ROWS), NEG, jnp.float32)
        stat[:, 1:2] = jnp.zeros((4, 1, ROWS), jnp.float32)
    else:
        acc[...] = acc_in[...]
        stat[...] = stat_in[...]

    def step(b, tiles, masks):
        scores = [nn(join(kvs, [tile], 0), qt[b]) for tile in tiles]
        if masks:
            scores = [jnp.where(mask, sc, NEG) for mask, sc in zip(masks, scores)]
        old = stat[b, 0:1]
        top = old
        for sc in scores:
            top = jnp.maximum(top, jnp.max(sc, axis=0, keepdims=True))
        fade = jnp.exp2((old - top) * CLOG)
        stat[b, 0:1] = top
        total = stat[b, 1:2] * fade
        out = acc[b] * fade
        for tile, sc in zip(tiles, scores):
            p = jnp.exp2((sc - top) * CLOG)
            total = total + jnp.sum(p, axis=0, keepdims=True)
            out = out + tn(join(kvs, [tile], 1), p.astype(BF))
        stat[b, 1:2] = total
        acc[b] = out

    visit(info, sources, step)
    if last:
        for b in range(4):
            out_t = acc[b] / stat[b, 1:2]
            o_ref[b] = out_t.T.astype(BF)
            row_ref[b, 0:1] = stat[b, 0:1] * CLOG + jnp.log2(stat[b, 1:2])
            prod = gt[b].astype(jnp.float32) * out_t.astype(BF).astype(jnp.float32)
            row_ref[b, 1:2] = jnp.sum(prod, axis=0, keepdims=True)


def bwd_kernel(sources, first, last, info, q, g, qt, gt, row, *refs):
    n = len(sources)
    if not first:
        dacc_in, refs = refs[0], refs[1:]
    kvs, refs = refs[: 2 * n], refs[2 * n:]
    if last:
        dq_ref, refs = refs[0], refs[1:]
        parts, dacc, dkvs = refs[: 2 * n], refs[2 * n], refs[2 * n + 1:]
    else:
        dacc, parts, dkvs = refs[0], refs[1: 2 * n + 1], refs[2 * n + 1:]
    dacc[...] = jnp.zeros_like(dacc) if first else dacc_in[...]
    for dkv in dkvs:
        dkv[...] = jnp.zeros_like(dkv)

    def step(b, tiles, masks):
        keys, vals = join(kvs, tiles, 0), join(kvs, tiles, 1)
        p = jnp.exp2(nn(keys, qt[b]) * CLOG - row[b, 0:1])
        if masks:
            p = jnp.where(join_masks(masks), p, 0.0)
        ds = (p * (nn(vals, gt[b]) - row[b, 1:2])).astype(BF)
        dacc[b] += tn(keys, ds)
        dk, dv = nn(ds, q[b]), nn(p.astype(BF), g[b])
        for k, (m, i, n) in enumerate(tiles):
            part = slice(k * TILE, (k + 1) * TILE)
            dkvs[m][i, n, 0] += dk[part]
            dkvs[m][i, n, 1] += dv[part]

    visit(info, sources, step)
    for m, (_, _, count) in enumerate(sources):
        def put(i, carry, m=m):
            for n in range(2):
                parts[2 * m + n][i, :, 0] = (dkvs[m][i, n, 0] * INV).astype(BF).reshape(4, 64, HDIM)
                parts[2 * m + n][i, :, 1] = dkvs[m][i, n, 1].astype(BF).reshape(4, 64, HDIM)
            return carry

        lax.fori_loop(0, count, put, 0)
    if last:
        for b in range(4):
            dq_ref[b] = (dacc[b] * INV).T.astype(BF)


def call(body, ins, outs, scratch, work, aliases={}):
    return pl.pallas_call(
        body,
        in_specs=[pl.BlockSpec(memory_space=pltpu.SMEM)] + [pl.BlockSpec(memory_space=pltpu.VMEM)] * (len(ins) - 1),
        out_specs=[pl.BlockSpec(memory_space=pltpu.VMEM)] * len(outs),
        out_shape=[jax.ShapeDtypeStruct(shape, dtype) for shape, dtype in outs],
        scratch_shapes=[pltpu.VMEM(shape, jnp.float32) for shape in scratch],
        compiler_params=pltpu.CompilerParams(vmem_limit_bytes=VMEM_LIMIT),
        input_output_aliases=aliases,
        cost_estimate=pl.CostEstimate(flops=work, bytes_accessed=4 << 20, transcendentals=0),
    )(*ins)


def fwd_part(info, qt, gt, state, blocks, last):
    sources = [(back, start, own.shape[0]) for back, start, own, _ in blocks]
    tiles = [ref for block in blocks for ref in block[2:]]
    kept = [((4, HDIM, ROWS), jnp.float32), ((4, 2, ROWS), jnp.float32)]
    outs = [((4, ROWS, HDIM), BF), kept[1]] if last else kept
    first = not state

    def body(*refs):
        fwd_kernel(sources, first, last, *refs)

    ins = [info, qt] + ([gt] if last else []) + list(state) + tiles
    return call(body, ins, outs, [shape for shape, _ in kept] if last else [], len(blocks) * 3_500_000_000,
                {2 + n: n for n in range(len(state))} if not last else {})


def bwd_part(info, q, g, qt, gt, row, state, blocks, last):
    sources = [(back, start, own.shape[0]) for back, start, own, _ in blocks]
    tiles = [ref for block in blocks for ref in block[2:]]
    acc = ((4, HDIM, ROWS), jnp.float32)
    parts = [(ref.shape, BF) for ref in tiles]
    sums = [(count, 2, 2, TILE, HDIM) for _, _, count in sources]
    first = not state

    def body(*refs):
        bwd_kernel(sources, first, last, *refs)

    outs = [((4, ROWS, HDIM), BF) if last else acc] + parts
    ins = [info, q, g, qt, gt, row] + list(state) + tiles
    return call(body, ins, outs, ([acc[0]] if last else []) + sums, len(blocks) * 5_000_000_000,
                {6: 0} if state and not last else {})


ALL = ("y", "z", "core", "x")
FWD_GROUPS = ((1, -1, 0), (2, -2), (3, -3))


def shift(value, axis, steps):
    count = SIZES[axis]
    return lax.ppermute(value, axis, [(i, (i + steps) % count) for i in range(count)])


def swap(value):
    return shift(value, "core", 1)


after = lax.optimization_barrier


def f32(value):
    return value.astype(jnp.float32)


def by_owner(value):
    return value.reshape(4, 16, 4, 8, HDIM).transpose(0, 2, 1, 3, 4).reshape(16, 128, HDIM)


def by_token(value):
    return value.reshape(4, 4, 16, 8, HDIM).transpose(0, 2, 1, 3, 4).reshape(64, 32, HDIM)


def shards(queries, key_states, value_states, out_grad, doc_lengths):
    y, z, core = (lax.axis_index(axis) for axis in ("y", "z", "core"))
    info = jnp.concatenate([jnp.stack([2 * z + core, y, z, core]), jnp.cumsum(doc_lengths)]).astype(jnp.int32)

    kv = jnp.stack([key_states, value_states]).transpose(2, 0, 1, 3)
    kv = jnp.broadcast_to(kv[None], (4, 4, 2, 64, HDIM)).reshape(16, 128, HDIM)
    own = lax.all_to_all(kv, ("y", "x"), 0, 0).reshape(4, 4, 2, 64, HDIM)
    q, g = by_owner(queries), by_owner(out_grad)

    blocks, state = {0: [(0, 0, own, swap(own))]}, []
    right = left = own
    for steps in (1, 2, 3, 4):
        if steps < 4:
            right, left = shift(right, "z", 1), shift(left, "z", -1)
        else:
            right, left = shift(right[:2], "z", 1), shift(left[2:], "z", -1)
        if steps == 1:
            q = lax.all_to_all(q, ("y", "x"), 0, 0)
            right, left, q = after((right, left, q))
            q = q.reshape(4, ROWS, HDIM)
            qt = q.transpose(0, 2, 1)
        else:
            chosen = [block for back in FWD_GROUPS[steps - 2] for block in blocks[back]]
            state = fwd_part(info, qt, None, state, chosen, False)
            if steps == 3:
                g = lax.all_to_all(g, ("y", "x"), 0, 0)
            right, left, state, g = after((right, left, state, g))
        if steps < 4:
            blocks[steps] = [(steps, 0, right, swap(right))]
            blocks[-steps] = [(-steps, 0, left, swap(left))]
        else:
            blocks[4] = [(4, 0, right, swap(right)), (4, 2, left, swap(left))]
    g = g.reshape(4, ROWS, HDIM)
    gt = g.transpose(0, 2, 1)
    out, row = fwd_part(info, qt, gt, state, blocks[4], True)
    out = out.reshape(16, 128, HDIM)

    def work(chosen, state, last):
        state, *sums = bwd_part(info, q, g, qt, gt, row, state, chosen, last)
        return [state], sums[0::2], sums[1::2]

    near = blocks[0][0][2:]
    halves = [(0, first, *(ref[first: first + 2] for ref in near)) for first in (0, 2)]
    state, mine, others = work(blocks[4], [], False)
    right, left = mine[0] + swap(others[0]), mine[1] + swap(others[1])
    state, right, left = after((state, right, left))
    here = []
    for steps in (3, 2, 1):
        from_left, from_right = shift(right, "z", 1), shift(left, "z", -1)
        chosen = blocks[-steps] + blocks[steps] + halves[:3 - steps][-1:]
        state, mine, others = work(chosen, state, steps == 1)
        state, others, from_left, from_right = after((state, others, from_left, from_right))
        right, left = mine[0] + swap(others[0]), mine[1] + swap(others[1])
        if steps == 3:
            right = jnp.concatenate([right[:2] + from_left, right[2:]])
            left = jnp.concatenate([left[:2], left[2:] + from_right])
        else:
            right, left = right + from_left, left + from_right
        here += [part + swap(other) for part, other in zip(mine[2:], others[2:])]
        state, right, left = after((state, right, left))
    from_left, from_right = shift(right, "z", 1), shift(left, "z", -1)
    here = jnp.concatenate(here)
    done = jnp.concatenate([out, state[0].reshape(16, 128, HDIM)], axis=1)
    done = lax.all_to_all(done, ("y", "x"), 0, 0)
    done, from_left, from_right = after((done, from_left, from_right))
    out, dq = by_token(done[:, :128]), by_token(done[:, 128:])

    dkv = (f32(here) + f32(from_left) + f32(from_right)).astype(BF).reshape(16, 2, 64, HDIM)
    dkv = lax.all_to_all(dkv, ("y", "x"), 0, 0).reshape(4, 4, 2, 64, HDIM)
    dkv = jnp.sum(f32(dkv), axis=0).astype(BF).transpose(1, 2, 0, 3)
    return out, dq, dkv[0], dkv[1]


def solution(mesh):
    fine = Mesh(mesh.devices.reshape(4, 8, 2, 4), ALL)
    return jax.shard_map(
        shards,
        mesh=fine,
        in_specs=(P(ALL), P(ALL), P(ALL), P(ALL), P()),
        out_specs=(P(ALL), P(ALL), P(ALL), P(ALL)),
        check_vma=False,
    )
```
